512 devices in a mesh: group: 4 (over z_hi), dp: 32 (over y, z_lo, core), tensor: 4 (over x).
Axes of the slice: x: 4, y: 4, z: 16 (z_hi: 4, z_lo: 4; z = z_hi * 4 + z_lo), core: 2. Of those that a mesh axis runs over, the one named last changes fastest.
Arguments:
- queries: bfloat16 [16384, 4096], P(('group', 'dp'), 'tensor'), may hold values from -16 to 16
- span_state: bfloat16 [16384, 4096], P(('group', 'dp'), 'tensor'), may hold values from -6 to 6
- neigh_state: bfloat16 [65536, 4096], P(('group', 'dp'), 'tensor'), may hold values from -24 to 24
- counts: int32 [4, 64], P('group'), may hold values from 1 to 2
- norm_gain: float32 [4096], P('tensor'), may hold values from 0.5 to 1.5
- head_gate: float32 [32], P('tensor'), may hold values from 0.3 to 1.5
- out_grad: bfloat16 [16384, 4096], P(('group', 'dp'), 'tensor'), may hold values from -6 to 6
Outputs:
- cross_output: bfloat16 [16384, 4096], P(('group', 'dp'), 'tensor')
- query_grad: bfloat16 [16384, 4096], P(('group', 'dp'), 'tensor')
- span_grad: bfloat16 [16384, 4096], P(('group', 'dp'), 'tensor')
- neighbour_grad: bfloat16 [65536, 4096], P(('group', 'dp'), 'tensor')
- gate_grad: float32 [32], P('tensor')
The draws below stay inside these ranges and needn't reach their ends.
Inputs may be any that keep to these rules, and one draw needn't show every extreme that they name: Slot j of span c holds a retrieved neighbour exactly when j < counts[c].
All inputs are finite; a program needn't handle non-finite values.
Results may differ from the reference program's by a relative error of at most 0.0095.
The reference program's roundings to bfloat16 on the way count: a program that leaves them out, or rounds other values in their place, can miss the bound.
Values may be sent and summed in bfloat16 or wider, within the bound.
No kernel may reach another device: no remote copies, remote signals or barrier semaphores. Data moves between devices by JAX's collectives and lax.ppermute only.
A program may use at most 64 MiB of HBM per device.

```python
import math
import jax
import jax.numpy as jnp
from jax import lax

HEADS = 32
HD = 128
CH = 64
NB = 2
NL = 128
HW = 4096
NCH = 64
LEN = 4096
SEQS = 4
TOKENS = 16384
NTOK = 65536


def column_scale(lowest, highest):
    fraction = jnp.arange(HW).astype(jnp.float32) / (HW - 1)
    return jnp.exp(jnp.log(lowest) + fraction * (jnp.log(highest) - jnp.log(lowest)))[None, :]


def draw_neigh_state(key, part):
    values = jax.random.normal(jax.random.fold_in(key, 7), (NTOK, HW), jnp.float32)
    values = values * column_scale(0.5, 2.0)
    return jnp.clip(values, -12.0, 12.0).astype(jnp.bfloat16)


def draw_queries(key, part):
    values = jax.random.normal(jax.random.fold_in(key, 9), (TOKENS, HW), jnp.float32)
    return jnp.clip(values, -6.0, 6.0).astype(jnp.bfloat16)


def with_ends(array, own_key, smallest, top_value):
    index_at = [jax.random.randint(jax.random.fold_in(own_key, axis), (), 0, length) for axis, length in enumerate(array.shape)]
    widest = array.shape.index(max(array.shape))
    next_to = index_at[:widest] + [(index_at[widest] + 1) % array.shape[widest]] + index_at[widest + 1:]
    return array.at[tuple(index_at)].set(smallest).at[tuple(next_to)].set(top_value)


def block_levels(rng, shape, pieces, smallest, largest):
    def one(axis_at, blocks):
        draws = jax.random.uniform(jax.random.fold_in(jax.random.fold_in(rng, 6), axis_at), (blocks,), jnp.float32, smallest / len(pieces), largest / len(pieces))
        return jnp.repeat(jnp.exp(draws), shape[axis_at] // blocks).reshape((-1,) + (1,) * (len(shape) - axis_at - 1))

    gain = one(*pieces[0])
    for cut in pieces[1:]:
        gain = gain * one(*cut)
    return gain


def bell_draw(stream_key, shape, scale, reach, pieces=(), held_as=jnp.bfloat16):
    entries = scale * jax.random.normal(stream_key, shape, jnp.float32)
    if pieces:
        entries = entries * block_levels(stream_key, shape, pieces, -0.22, 0.18)
    return jnp.clip(entries, -reach, reach).astype(held_as)


def setup_inputs(seed: int = 0) -> dict:
    key_of = jax.random.split(jax.random.key(seed), 8)
    return {
        "queries": draw_queries(jax.random.fold_in(key_of[7], 71), 0),
        "span_state": bell_draw(key_of[1], (TOKENS, HW), 1.0, 6.0, ((0, 128), (1, 4))),
        "neigh_state": draw_neigh_state(jax.random.fold_in(key_of[7], 71), 0),
        "counts": with_ends(jax.random.randint(key_of[3], (SEQS, NCH), 1, NB + 1), jax.random.fold_in(key_of[3], 1), 1, NB).astype(jnp.int32),
        "norm_gain": jnp.clip(1.0 + 0.1 * jax.random.normal(key_of[4], (HW,), jnp.float32), 0.5, 1.5),
        "head_gate": jnp.clip(0.3 + 1.2 * jax.random.uniform(key_of[5], (HEADS,), jnp.float32) ** block_levels(key_of[5], (HEADS,), ((0, 4),), -0.2, 0.2), 0.3, 1.5),
        "out_grad": bell_draw(key_of[6], (TOKENS, HW), 1.0, 6.0, ((0, 128), (1, 4))),
    }


epsilon = 1e-05
masked_score = -1e+30

def product(form, left, right):
    return jnp.einsum(form, left.astype(jnp.float32), right.astype(jnp.float32))

def encoder_forward(normed, neighbours, contexts):
    slot_count = normed.shape[1]
    spread = jnp.broadcast_to(contexts[:, None], (contexts.shape[0], slot_count) + contexts.shape[1:])
    all_keys = jnp.concatenate([normed, spread], axis=2)
    scores = product('cjqhd,cjkhd->cjhqk', normed, all_keys) / normed.shape[-1]
    powers = jnp.exp(scores)
    weights = powers / lax.optimization_barrier(jnp.sum(powers, axis=-1, keepdims=True))
    rounded = weights.astype(jnp.bfloat16)
    mixture = product('cjhqk,cjkhd->cjqhd', rounded, all_keys)
    encoded = (neighbours.astype(jnp.float32) + mixture).astype(jnp.bfloat16)
    return (encoded, (all_keys, weights, rounded, mixture))

def encoder_backward(grad_encoded, normed, saved):
    all_keys, weights, rounded, mixture = saved
    grad_rounded = grad_encoded.astype(jnp.bfloat16)
    grad_weights = product('cjqhd,cjkhd->cjhqk', grad_rounded, all_keys)
    offset = jnp.moveaxis(lax.optimization_barrier(jnp.sum(grad_encoded * mixture, axis=-1)), -1, 2)[..., None]
    score_grad = (weights * (grad_weights - offset) / normed.shape[-1]).astype(jnp.bfloat16)
    normed_grad = product('cjhqk,cjkhd->cjqhd', score_grad, all_keys)
    key_grad = product('cjhqk,cjqhd->cjkhd', score_grad, normed) + product('cjhqk,cjqhd->cjkhd', rounded, grad_rounded)
    length = normed.shape[2]
    normed_grad = normed_grad + key_grad[:, :, :length]
    context_grad = lax.optimization_barrier(jnp.sum(key_grad[:, :, length:], axis=1))
    return (normed_grad, context_grad)

def cross_attend(blocks, grad_blocks, keys, usable, present, gate_tanh):
    scale = 1.0 / math.sqrt(blocks.shape[-1])
    scores = product('brhd,bmhd->bhrm', blocks, keys) * scale
    scores = jnp.where(usable[:, None, None, :], scores, masked_score)
    highest = lax.optimization_barrier(jnp.max(scores, axis=-1, keepdims=True))
    powers = jnp.exp(scores - highest)
    weights = powers / lax.optimization_barrier(jnp.sum(powers, axis=-1, keepdims=True))
    rounded = weights.astype(jnp.bfloat16)
    attended = product('bhrm,bmhd->brhd', rounded, keys)
    present_mask = present[:, None, None, None]
    attended = jnp.where(present_mask, attended, 0.0)
    output = (gate_tanh[:, None] * attended).astype(jnp.bfloat16)
    grad_output = grad_blocks.astype(jnp.float32)
    gate_term = lax.optimization_barrier(jnp.sum(grad_output * attended, axis=(0, 1, 3)))
    att_grad = jnp.where(present_mask, gate_tanh[:, None] * grad_output, 0.0)
    grad_rounded = att_grad.astype(jnp.bfloat16)
    grad_weights = product('brhd,bmhd->bhrm', grad_rounded, keys)
    offset = jnp.moveaxis(lax.optimization_barrier(jnp.sum(att_grad * attended, axis=-1)), -1, 1)[..., None]
    score_grad = (weights * (grad_weights - offset) * scale).astype(jnp.bfloat16)
    query_grad = product('bhrm,bmhd->brhd', score_grad, keys).astype(jnp.bfloat16)
    key_grad = product('bhrm,brhd->bmhd', score_grad, blocks) + product('bhrm,brhd->bmhd', rounded, grad_rounded)
    return (output, query_grad, key_grad, gate_term)

def reference(queries, span_state, neigh_state, counts, norm_gain, head_gate, out_grad):
    total_spans = SEQS * NCH
    lead = CH - 1

    def shifted(matrix):
        per_sequence = matrix.reshape(SEQS, LEN, HW)
        padding = jnp.zeros((SEQS, lead, HW), matrix.dtype)
        joined = jnp.concatenate([per_sequence[:, lead:], padding], axis=1)
        return joined.reshape(total_spans, CH, HEADS, HD)
    blocks = shifted(queries)
    grad_blocks = shifted(out_grad)
    neighbours = neigh_state.reshape(total_spans, NB, NL, HEADS, HD)
    contexts = span_state.reshape(total_spans, CH, HEADS, HD)
    flat_counts = counts.reshape(total_spans).astype(jnp.int32)
    gains = norm_gain.reshape(HEADS, HD)
    gate_tanh = jnp.tanh(head_gate)

    def one_span(items):
        block, grad_block, neighbour, context, count = items
        neighbour = neighbour[None]
        floats = neighbour.astype(jnp.float32)
        square_sum = lax.optimization_barrier(jnp.sum(floats * floats, axis=(3, 4)))
        inverse = lax.rsqrt(square_sum / (HEADS * HD) + epsilon)[..., None, None]
        scaled = floats * inverse
        normed = (scaled * gains).astype(jnp.bfloat16)
        encoded, saved = encoder_forward(normed, neighbour, context[None])
        keys = encoded.reshape(1, NB * NL, HEADS, HD)
        usable = jnp.repeat(jnp.arange(NB) < count, NL)[None]
        present = (count > 0)[None]
        output, query_grad, key_grad, gate_term = cross_attend(block[None], grad_block[None], keys, usable, present, gate_tanh)
        grad_encoded = key_grad.reshape(1, NB, NL, HEADS, HD)
        normed_grad, context_grad = encoder_backward(grad_encoded, normed, saved)
        gain_grad = normed_grad * gains
        projection = lax.optimization_barrier(jnp.sum(gain_grad * scaled, axis=(3, 4))) / (HEADS * HD)
        neighbour_grad = grad_encoded + inverse * (gain_grad - scaled * projection[..., None, None])
        return (output[0], query_grad[0], context_grad[0].astype(jnp.bfloat16), neighbour_grad[0].astype(jnp.bfloat16), gate_term)
    results = lax.map(one_span, (blocks, grad_blocks, neighbours, contexts, flat_counts))
    out_blocks, grad_rows, context_rows, neighbour_rows, gate_terms = results

    def unshift(stacked):
        per_sequence = stacked.reshape(SEQS, LEN, HW)
        padding = jnp.zeros((SEQS, lead, HW), stacked.dtype)
        joined = jnp.concatenate([padding, per_sequence], axis=1)[:, :LEN]
        return joined.reshape(TOKENS, HW)
    cross_output = unshift(out_blocks)
    query_grad = unshift(grad_rows)
    span_grad = context_rows.reshape(TOKENS, HW)
    neighbour_grad = neighbour_rows.reshape(NTOK, HW)
    gate_grad = (1.0 - gate_tanh * gate_tanh) * lax.optimization_barrier(jnp.sum(gate_terms, axis=0)) / math.sqrt(TOKENS)
    return (cross_output, query_grad, span_grad, neighbour_grad, gate_grad)
```

```python
import functools
import math

import jax
import jax.numpy as jnp
from jax import lax
from jax.experimental import pallas as pl
from jax.experimental.pallas import tpu as pltpu
from jax.sharding import PartitionSpec as P

CH = 64
NB = 2
NL = 128
HD = 128
KEYS = NL + CH
EPSILON = 1e-05
MASKED = -1e30
VMEM_LIMIT = 48 * 1024 * 1024

f32 = jnp.float32
bf16 = jnp.bfloat16


def dot(left, right, left_dim, right_dim):
    return lax.dot_general(
        left, right, (((left_dim,), (right_dim,)), ((), ())), preferred_element_type=f32
    )


def cost(flops, nbytes):
    return pl.CostEstimate(flops=flops, bytes_accessed=nbytes, transcendentals=0)


def columns(row):
    return jnp.transpose(jnp.broadcast_to(row, (NL, NL)))


def row_sums(block):
    return jnp.sum(jnp.transpose(block), axis=0, keepdims=True)


def inverse_rows(square_ref, full_width):
    total = (square_ref[0] + square_ref[1]) + (square_ref[2] + square_ref[3])
    return lax.rsqrt(total / full_width + EPSILON)


def squares_kernel(x_ref, q_ref, o_ref, sum_ref, pack_ref):
    step = pl.program_id(0)
    width = x_ref.shape[1]
    total = jnp.zeros((NL, HD), f32)
    for at in range(0, width, HD):
        part = x_ref[:, at : at + HD].astype(f32)
        total = total + part * part
    row = row_sums(total)
    for device in range(sum_ref.shape[0]):
        sum_ref[device, pl.ds(step, 1), :] = row

    @pl.when(step == 0)
    def _():
        pack_ref[0:CH, :] = q_ref[...]
        pack_ref[CH : 2 * CH, :] = o_ref[...]


def squares(x, queries, out_grad, ranks):
    rows, width = x.shape
    count = rows // NL
    half = pl.BlockSpec((CH, width), lambda i: (0, 0))
    return pl.pallas_call(
        squares_kernel,
        grid=(count,),
        in_specs=[pl.BlockSpec((NL, width), lambda i: (i, 0)), half, half],
        out_specs=[
            pl.BlockSpec((ranks, count, NL), lambda i: (0, 0, 0)),
            pl.BlockSpec((2 * CH, width), lambda i: (0, 0)),
        ],
        out_shape=[
            jax.ShapeDtypeStruct((ranks, count, NL), f32),
            jax.ShapeDtypeStruct((2 * CH, width), bf16),
        ],
        cost_estimate=cost(2 * rows * width, 2 * rows * width),
    )(x, queries, out_grad)


def cross(block, grad_block, keys, count, gate_row):
    scale = 1.0 / math.sqrt(HD)
    lane = lax.broadcasted_iota(jnp.int32, (CH, NB * NL), 1)
    scores = dot(block, keys, 1, 1) * scale
    scores = jnp.where(lane < count * NL, scores, MASKED)
    highest = jnp.max(scores, axis=-1, keepdims=True)
    powers = jnp.exp(scores - highest)
    weights = powers * (1.0 / jnp.sum(powers, axis=-1, keepdims=True))
    rounded = weights.astype(bf16)
    present = count > 0
    attended = jnp.where(present, dot(rounded, keys, 1, 0), 0.0)
    output = gate_row * attended
    term = jnp.sum(grad_block * attended, axis=0, keepdims=True)
    att_grad = jnp.where(present, gate_row * grad_block, 0.0)
    att_rounded = att_grad.astype(bf16)
    grad_weights = dot(att_rounded, keys, 1, 1)
    offset = jnp.sum(att_grad * attended, axis=-1, keepdims=True)
    score_grad = (weights * (grad_weights - offset) * scale).astype(bf16)
    query_grad = dot(score_grad, keys, 1, 0)
    key_grad = dot(
        jnp.concatenate([score_grad, rounded], axis=0),
        jnp.concatenate([block, att_rounded], axis=0),
        0,
        0,
    )
    return output, query_grad, key_grad, term


def forward_kernel(
    full_width,
    counts_ref,
    gate_ref,
    square_ref,
    gain_ref,
    x_ref,
    context_ref,
    q_ref,
    o_ref,
    next_q_ref,
    next_o_ref,
    normed_ref,
    prob_ref,
    grad_ref,
    out_ref,
    query_ref,
    back_ref,
    term_ref,
    inverse_ref,
):
    head = pl.program_id(0)
    slots = x_ref.shape[0] // NL
    spans = slots // NB

    @pl.when(head == 0)
    def _():
        inverse = inverse_rows(square_ref, full_width)
        for n in range(slots):
            inverse_ref[n * NL : (n + 1) * NL, :] = columns(inverse[n : n + 1, :])
        term_ref[...] = jnp.zeros_like(term_ref)

    gain = gain_ref[...]
    gate_row = jnp.tanh(jnp.full((1, HD), gate_ref[head], f32))
    encoded = []
    for n in range(slots):
        rows = slice(n * NL, (n + 1) * NL)
        span = n // NB
        x = x_ref[rows, :].astype(f32)
        normed = ((x * inverse_ref[rows, :]) * gain).astype(bf16)
        normed_ref[rows, :] = normed
        keys = jnp.concatenate([normed, context_ref[span * CH : (span + 1) * CH, :]], axis=0)
        powers = jnp.exp(dot(keys, normed, 1, 1) * (1.0 / HD))
        total = jnp.sum(powers, axis=0, keepdims=True)
        rounded = (powers * (1.0 / total)).astype(bf16)
        prob_ref[n] = rounded
        encoded.append((x + dot(rounded, keys, 0, 0)).astype(bf16))

    last = lax.broadcasted_iota(jnp.int32, (CH, HD), 0) == CH - 1

    def blocks(own_ref, next_ref):
        own = own_ref[...].astype(f32)
        following = next_ref[...].astype(f32)
        first = jnp.where(last, own[CH - 1 : CH, :], own[CH:, :])
        second = jnp.where(last, own[2 * CH - 1 :, :], following)
        return first, second

    q_blocks = blocks(q_ref, next_q_ref)
    o_blocks = blocks(o_ref, next_o_ref)
    outs, queries, terms = [], [], []
    for span in range(spans):
        keys = jnp.concatenate(encoded[span * NB : (span + 1) * NB], axis=0)
        output, query_grad, key_grad, term = cross(
            q_blocks[span].astype(bf16), o_blocks[span], keys, counts_ref[span], gate_row
        )
        grad_ref[span * NB * NL : (span + 1) * NB * NL, :] = key_grad
        outs.append(output)
        queries.append(query_grad)
        terms.append(term)
    for at, (target, pair) in enumerate(((out_ref, outs), (query_ref, queries))):
        first, second = pair
        target[0:CH, :] = jnp.broadcast_to(first[CH - 1 :, :], (CH, HD)).astype(bf16)
        target[CH:, :] = jnp.where(last, second[CH - 1 :, :], first).astype(bf16)
        back_ref[at * CH : (at + 1) * CH, :] = second.astype(bf16)
    lane = lax.broadcasted_iota(jnp.int32, (1, HD), 1)
    value = jnp.sum(terms[0] + terms[1], axis=-1, keepdims=True)
    term_ref[...] += jnp.where(lane == head, value, 0.0)


def forward(own_counts, head_gate, squares_all, gain, x, context, queries, out_grad, arrived, full_width):
    rows, width = x.shape
    heads = width // HD
    tokens = queries.shape[0]
    slots = rows // NL

    def tall(size):
        return pl.BlockSpec((size, HD), lambda h: (0, h))

    smem = pl.BlockSpec(memory_space=pltpu.SMEM)
    return pl.pallas_call(
        functools.partial(forward_kernel, full_width),
        grid=(heads,),
        in_specs=[
            smem,
            smem,
            pl.BlockSpec(squares_all.shape, lambda h: (0, 0, 0)),
            pl.BlockSpec((1, HD), lambda h: (0, h)),
            tall(rows),
            tall(tokens),
            tall(tokens),
            tall(tokens),
            tall(CH),
            pl.BlockSpec((CH, HD), lambda h: (1, h)),
        ],
        out_specs=[
            tall(rows),
            pl.BlockSpec((None, slots, KEYS, NL), lambda h: (h, 0, 0, 0)),
            tall(rows),
            tall(tokens),
            tall(tokens),
            tall(tokens),
            pl.BlockSpec((1, HD), lambda h: (0, 0)),
        ],
        out_shape=[
            jax.ShapeDtypeStruct((rows, width), bf16),
            jax.ShapeDtypeStruct((heads, slots, KEYS, NL), bf16),
            jax.ShapeDtypeStruct((rows, width), f32),
            jax.ShapeDtypeStruct((tokens, width), bf16),
            jax.ShapeDtypeStruct((tokens, width), bf16),
            jax.ShapeDtypeStruct((tokens, width), bf16),
            jax.ShapeDtypeStruct((1, HD), f32),
        ],
        scratch_shapes=[pltpu.VMEM((rows, HD), f32)],
        compiler_params=pltpu.CompilerParams(vmem_limit_bytes=VMEM_LIMIT),
        cost_estimate=cost(4 * 10**9, 10**7),
    )(own_counts, head_gate, squares_all, gain, x, context, queries, out_grad, arrived, arrived)


def backward_kernel(
    full_width,
    square_ref,
    gain_ref,
    x_ref,
    context_ref,
    normed_ref,
    prob_ref,
    grad_ref,
    mid_ref,
    context_grad_ref,
    project_ref,
    inverse_ref,
    total_ref,
):
    head = pl.program_id(0)
    slots = x_ref.shape[0] // NL

    @pl.when(head == 0)
    def _():
        inverse = inverse_rows(square_ref, full_width)
        for n in range(slots):
            inverse_ref[n * NL : (n + 1) * NL, :] = columns(inverse[n : n + 1, :])
        total_ref[...] = jnp.zeros_like(total_ref)

    gain = gain_ref[...]
    context_sum = None
    for n in range(slots):
        rows = slice(n * NL, (n + 1) * NL)
        span = n // NB
        normed = normed_ref[rows, :]
        keys = jnp.concatenate([normed, context_ref[span * CH : (span + 1) * CH, :]], axis=0)
        grad = grad_ref[rows, :]
        grad_rounded = grad.astype(bf16)
        prob = prob_ref[n]
        weights = prob.astype(f32)
        grad_weights = dot(keys, grad_rounded, 1, 1)
        offset = jnp.sum(weights * grad_weights, axis=0, keepdims=True)
        score_grad = (weights * (grad_weights - offset) * (1.0 / HD)).astype(bf16)
        key_grad = dot(
            jnp.concatenate([score_grad, prob], axis=1),
            jnp.concatenate([normed, grad_rounded], axis=0),
            1,
            0,
        )
        normed_grad = dot(score_grad, keys, 0, 0) + key_grad[:NL, :]
        gained = normed_grad * gain
        inverse = inverse_ref[rows, :]
        scaled = x_ref[rows, :].astype(f32) * inverse
        total_ref[rows, :] += gained * scaled
        mid_ref[rows, :] = grad + inverse * gained
        part = key_grad[NL:, :]
        if n % NB == 0:
            context_sum = part
        else:
            context_grad_ref[span * CH : (span + 1) * CH, :] = (context_sum + part).astype(bf16)

    @pl.when(head == pl.num_programs(0) - 1)
    def _():
        for n in range(slots):
            row = row_sums(total_ref[n * NL : (n + 1) * NL, :])
            for device in range(project_ref.shape[0]):
                project_ref[device, n : n + 1, :] = row


def backward(squares_all, gain, x, context, normed, prob, grad, full_width):
    rows, width = x.shape
    heads = width // HD
    tokens = context.shape[0]
    slots = rows // NL

    def tall(size):
        return pl.BlockSpec((size, HD), lambda h: (0, h))

    whole = pl.BlockSpec(squares_all.shape, lambda h: (0, 0, 0))
    return pl.pallas_call(
        functools.partial(backward_kernel, full_width),
        grid=(heads,),
        in_specs=[
            whole,
            pl.BlockSpec((1, HD), lambda h: (0, h)),
            tall(rows),
            tall(tokens),
            tall(rows),
            pl.BlockSpec((None, slots, KEYS, NL), lambda h: (h, 0, 0, 0)),
            tall(rows),
        ],
        out_specs=[tall(rows), tall(tokens), whole],
        out_shape=[
            jax.ShapeDtypeStruct((rows, width), f32),
            jax.ShapeDtypeStruct((tokens, width), bf16),
            jax.ShapeDtypeStruct(squares_all.shape, f32),
        ],
        scratch_shapes=[pltpu.VMEM((rows, HD), f32), pltpu.VMEM((rows, HD), f32)],
        compiler_params=pltpu.CompilerParams(vmem_limit_bytes=VMEM_LIMIT),
        cost_estimate=cost(4 * 10**9, 10**7),
    )(squares_all, gain, x, context, normed, prob, grad)


def final_kernel(
    full_width,
    square_ref,
    project_ref,
    x_ref,
    mid_ref,
    out_in_ref,
    query_in_ref,
    ret_out_ref,
    ret_query_ref,
    grad_ref,
    out_ref,
    query_ref,
    factor_ref,
):
    step = pl.program_id(0)
    slots = x_ref.shape[0] // NL

    @pl.when(step == 0)
    def _():
        inverse = inverse_rows(square_ref, full_width)
        project = (project_ref[0] + project_ref[1]) + (project_ref[2] + project_ref[3])
        factor = inverse * inverse * (project / full_width)
        for n in range(slots):
            factor_ref[n * NL : (n + 1) * NL, :] = columns(factor[n : n + 1, :])

    width = x_ref.shape[1]
    factor = factor_ref[...]
    for at in range(0, width, HD):
        cols = slice(at, at + HD)
        x = x_ref[:, cols].astype(f32)
        grad_ref[:, cols] = (mid_ref[:, cols] - x * factor).astype(bf16)
    last = lax.broadcasted_iota(jnp.int32, (CH, width), 0) == CH - 1
    for own, back, target in (
        (out_in_ref, ret_out_ref, out_ref),
        (query_in_ref, ret_query_ref, query_ref),
    ):
        own_rows = own[...].astype(f32)
        target[...] = jnp.where(last, own_rows, back[...].astype(f32)).astype(bf16)


def final(squares_all, projects_all, x, mid, out, query, returned, full_width):
    rows, width = x.shape
    tokens = out.shape[0]
    part = 2 * HD
    whole = pl.BlockSpec(squares_all.shape, lambda i: (0, 0, 0))
    tall = pl.BlockSpec((rows, part), lambda i: (0, i))
    half = pl.BlockSpec((CH, part), lambda i: (0, i))
    return pl.pallas_call(
        functools.partial(final_kernel, full_width),
        grid=(width // part,),
        in_specs=[
            whole,
            whole,
            tall,
            tall,
            half,
            half,
            half,
            pl.BlockSpec((CH, part), lambda i: (1, i)),
        ],
        out_specs=[tall, half, half],
        out_shape=[
            jax.ShapeDtypeStruct((rows, width), bf16),
            jax.ShapeDtypeStruct((tokens, width), bf16),
            jax.ShapeDtypeStruct((tokens, width), bf16),
        ],
        scratch_shapes=[pltpu.VMEM((rows, HD), f32)],
        input_output_aliases={4: 1, 5: 2},
        compiler_params=pltpu.CompilerParams(vmem_limit_bytes=VMEM_LIMIT),
        cost_estimate=cost(4 * rows * width, 8 * rows * width),
    )(squares_all, projects_all, x, mid, out, query, returned, returned)


def shards(queries, span_state, neigh_state, counts, norm_gain, head_gate, out_grad):
    head_count = head_gate.shape[0]
    width = queries.shape[1]
    row_count = queries.shape[0]
    span_count = row_count // CH
    ranks = lax.axis_size("tensor")
    full_width = float(ranks * width)
    lines = lax.axis_size("dp")

    local_squares, pack = squares(neigh_state, queries, out_grad, ranks)
    arrived = lax.ppermute(pack, "dp", [(i, i - 1) for i in range(1, lines)])
    squares_all = lax.all_to_all(local_squares, "tensor", 0, 0, tiled=True)
    gain = norm_gain[None, :]
    first_span = lax.axis_index("dp") * span_count
    own_counts = lax.dynamic_slice_in_dim(counts.reshape(-1), first_span, span_count)
    normed, prob, grad, out, query, back, term = forward(
        own_counts, head_gate, squares_all, gain, neigh_state, span_state, queries, out_grad,
        arrived, full_width,
    )
    gathered = lax.all_to_all(jnp.broadcast_to(term, (lines, HD)), "dp", 0, 0, tiled=True)
    summed = jnp.sum(gathered, axis=0)
    returned = lax.ppermute(back, "dp", [(i, i + 1) for i in range(lines - 1)])
    mid, context_grad, local_project = backward(
        squares_all, gain, neigh_state, span_state, normed, prob, grad, full_width
    )
    projects_all = lax.all_to_all(local_project, "tensor", 0, 0, tiled=True)
    for step in (1, 2):
        count = lax.axis_size("group")
        summed = summed + lax.ppermute(summed, "group", [(i, i ^ step) for i in range(count)])
    neighbour_grad, out, query = final(
        squares_all, projects_all, neigh_state, mid, out, query, returned, full_width
    )
    gate_tanh = jnp.tanh(head_gate)
    total_tokens = lax.axis_size("group") * lines * row_count
    gate_grad = (1.0 - gate_tanh * gate_tanh) * summed[:head_count] / math.sqrt(total_tokens)
    return out, query, context_grad, neighbour_grad, gate_grad


def solution(mesh):
    rows = P(("group", "dp"), "tensor")
    return jax.shard_map(
        shards,
        mesh=mesh,
        in_specs=(rows, rows, rows, P("group", None), P("tensor"), P("tensor"), rows),
        out_specs=(rows, rows, rows, rows, P("tensor")),
        check_vma=False,
    )
```

```python
import functools
import math

import jax
import jax.numpy as jnp
from jax import lax
from jax.experimental import pallas as pl
from jax.experimental.pallas import tpu as pltpu
from jax.sharding import PartitionSpec as P

CH = 64
NB = 2
NL = 128
HD = 128
KEYS = NL + CH
EPSILON = 1e-05
MASKED = -1e30
VMEM_LIMIT = 61 * 1024 * 1024
HEADS_PER_STEP = 4
SIDE_BY_SIDE = 4

f32 = jnp.float32
bf16 = jnp.bfloat16


def dot(left, right, left_dim, right_dim):
    return lax.dot_general(
        left, right, (((left_dim,), (right_dim,)), ((), ())), preferred_element_type=f32
    )


def cost(flops, nbytes):
    return pl.CostEstimate(flops=flops, bytes_accessed=nbytes, transcendentals=0)


def columns(row):
    return jnp.transpose(jnp.broadcast_to(row, (NL, NL)))


def row_sums(block):
    return jnp.sum(jnp.transpose(block), axis=0, keepdims=True)


def inverse_rows(square_ref, full_width):
    total = (square_ref[0] + square_ref[1]) + (square_ref[2] + square_ref[3])
    return lax.rsqrt(total / full_width + EPSILON)


def squares_kernel(x_ref, q_ref, o_ref, sum_ref, pack_ref):
    step = pl.program_id(0)
    width = x_ref.shape[1]
    total = jnp.zeros((NL, HD), f32)
    for at in range(0, width, HD):
        part = x_ref[:, at : at + HD].astype(f32)
        total = total + part * part
    row = row_sums(total)
    for device in range(sum_ref.shape[0]):
        sum_ref[device, pl.ds(step, 1), :] = row

    @pl.when(step == 0)
    def _():
        pack_ref[0:CH, :] = q_ref[...]
        pack_ref[CH : 2 * CH, :] = o_ref[...]


def squares(x, queries, out_grad, ranks):
    rows, width = x.shape
    count = rows // NL
    half = pl.BlockSpec((CH, width), lambda i: (0, 0))
    return pl.pallas_call(
        squares_kernel,
        grid=(count,),
        in_specs=[pl.BlockSpec((NL, width), lambda i: (i, 0)), half, half],
        out_specs=[
            pl.BlockSpec((ranks, count, NL), lambda i: (0, 0, 0)),
            pl.BlockSpec((2 * CH, width), lambda i: (0, 0)),
        ],
        out_shape=[
            jax.ShapeDtypeStruct((ranks, count, NL), f32),
            jax.ShapeDtypeStruct((2 * CH, width), bf16),
        ],
        cost_estimate=cost(2 * rows * width, 2 * rows * width),
    )(x, queries, out_grad)


def cross(items):
    scale = 1.0 / math.sqrt(HD)
    lane = lax.broadcasted_iota(jnp.int32, (CH, NB * NL), 1)
    scores = [dot(block, keys, 1, 1) * scale for block, _, keys, _, _ in items]
    scores = [jnp.where(lane < it[3] * NL, sc, MASKED) for it, sc in zip(items, scores)]
    highest = [jnp.max(sc, axis=-1, keepdims=True) for sc in scores]
    powers = [jnp.exp(sc - hi) for sc, hi in zip(scores, highest)]
    sums = [jnp.sum(po, axis=-1, keepdims=True) for po in powers]
    weights = [po * (1.0 / su) for po, su in zip(powers, sums)]
    rounded = [we.astype(bf16) for we in weights]
    attended = [dot(ro, it[2], 1, 0) for it, ro in zip(items, rounded)]
    attended = [jnp.where(it[3] > 0, at, 0.0) for it, at in zip(items, attended)]
    att_grad = [jnp.where(it[3] > 0, it[4] * it[1], 0.0) for it in items]
    att_rounded = [ag.astype(bf16) for ag in att_grad]
    grad_weights = [dot(ar, it[2], 1, 1) for it, ar in zip(items, att_rounded)]
    offset = [jnp.sum(ag * at, axis=-1, keepdims=True) for ag, at in zip(att_grad, attended)]
    score_grad = [
        (we * (gw - of) * scale).astype(bf16) for we, gw, of in zip(weights, grad_weights, offset)
    ]
    query_grad = [dot(sg, it[2], 1, 0) for it, sg in zip(items, score_grad)]
    key_grad = [
        dot(
            jnp.concatenate([sg, ro], axis=0),
            jnp.concatenate([it[0], ar], axis=0),
            0,
            0,
        )
        for it, sg, ro, ar in zip(items, score_grad, rounded, att_rounded)
    ]
    outputs = [it[4] * at for it, at in zip(items, attended)]
    terms = [jnp.sum(it[1] * at, axis=0, keepdims=True) for it, at in zip(items, attended)]
    return outputs, query_grad, key_grad, terms


def main_kernel(
    full_width,
    counts_ref,
    gate_ref,
    square_ref,
    gain_ref,
    x_ref,
    context_ref,
    q_ref,
    o_ref,
    next_q_ref,
    next_o_ref,
    mid_ref,
    out_ref,
    query_ref,
    back_ref,
    context_grad_ref,
    project_ref,
    term_ref,
    inverse_ref,
    total_ref,
):
    step = pl.program_id(0)
    slots = x_ref.shape[0] // NL
    spans = slots // NB

    @pl.when(step == 0)
    def _():
        inverse = inverse_rows(square_ref, full_width)
        for n in range(slots):
            inverse_ref[n * NL : (n + 1) * NL, :] = columns(inverse[n : n + 1, :])
        total_ref[...] = jnp.zeros_like(total_ref)
        term_ref[...] = jnp.zeros_like(term_ref)

    last = lax.broadcasted_iota(jnp.int32, (CH, HD), 0) == CH - 1
    lane = lax.broadcasted_iota(jnp.int32, (1, HD), 1)

    def blocks(own_ref, next_ref, cols):
        own = own_ref[:, cols].astype(f32)
        following = next_ref[:, cols].astype(f32)
        first = jnp.where(last, own[CH - 1 : CH, :], own[CH:, :])
        second = jnp.where(last, own[2 * CH - 1 :, :], following)
        return first, second

    def several(inners):
        heads = [(inner, step * HEADS_PER_STEP + inner) for inner in inners]
        cols = {inner: slice(inner * HD, (inner + 1) * HD) for inner in inners}
        gains = {inner: gain_ref[:, cols[inner]] for inner in inners}
        gates = {inner: jnp.tanh(jnp.full((1, HD), gate_ref[head], f32)) for inner, head in heads}
        pairs = [(inner, n) for inner in inners for n in range(slots)]
        rows = [slice(n * NL, (n + 1) * NL) for n in range(slots)]
        xs = [x_ref[rows[n], cols[i]].astype(f32) for i, n in pairs]
        scaled = [x * inverse_ref[rows[n], :] for x, (i, n) in zip(xs, pairs)]
        normed = [(sc * gains[i]).astype(bf16) for sc, (i, n) in zip(scaled, pairs)]
        keys = [
            jnp.concatenate([no, context_ref[n // NB * CH : (n // NB + 1) * CH, cols[i]]], axis=0)
            for no, (i, n) in zip(normed, pairs)
        ]
        powers = [jnp.exp(dot(ke, no, 1, 1) * (1.0 / HD)) for ke, no in zip(keys, normed)]
        totals = [1.0 / jnp.sum(po, axis=0, keepdims=True) for po in powers]
        weights = [po * to for po, to in zip(powers, totals)]
        probs = [we.astype(bf16) for we in weights]
        encoded = [
            (x + dot(pr, ke, 0, 0)).astype(bf16) for x, pr, ke in zip(xs, probs, keys)
        ]
        items = []
        for inner in inners:
            q_blocks = blocks(q_ref, next_q_ref, cols[inner])
            o_blocks = blocks(o_ref, next_o_ref, cols[inner])
            for span in range(spans):
                first = inners.index(inner) * slots + span * NB
                items.append((
                    q_blocks[span].astype(bf16), o_blocks[span],
                    jnp.concatenate(encoded[first : first + NB], axis=0),
                    counts_ref[span], gates[inner],
                ))
        outputs, query_grads, span_grads, terms = cross(items)
        grads = [
            span_grads[k // NB][k % NB * NL : (k % NB + 1) * NL, :] for k in range(len(pairs))
        ]
        grad_rounded = [gr.astype(bf16) for gr in grads]
        grad_weights = [dot(ke, gr, 1, 1) for ke, gr in zip(keys, grad_rounded)]
        offsets = [jnp.sum(we * gw, axis=0, keepdims=True) for we, gw in zip(weights, grad_weights)]
        score_grads = [
            (we * (gw - of) * (1.0 / HD)).astype(bf16)
            for we, gw, of in zip(weights, grad_weights, offsets)
        ]
        key_grads = [
            dot(
                jnp.concatenate([sg, pr], axis=1),
                jnp.concatenate([no, gr], axis=0),
                1,
                0,
            )
            for sg, pr, no, gr in zip(score_grads, probs, normed, grad_rounded)
        ]
        gained = [
            (dot(sg, ke, 0, 0) + kg[:NL, :]) * gains[i]
            for sg, ke, kg, (i, n) in zip(score_grads, keys, key_grads, pairs)
        ]
        sums = [None] * slots
        for k, (i, n) in enumerate(pairs):
            product = gained[k] * scaled[k]
            sums[n] = product if sums[n] is None else sums[n] + product
            mid_ref[rows[n], cols[i]] = grads[k] + inverse_ref[rows[n], :] * gained[k]
            if n % NB == NB - 1:
                context_grad_ref[n // NB * CH : (n // NB + 1) * CH, cols[i]] = (
                    key_grads[k - 1][NL:, :] + key_grads[k][NL:, :]
                ).astype(bf16)
        for n in range(slots):
            total_ref[rows[n], :] += sums[n]
        result = jnp.zeros((1, HD), f32)
        for at, (inner, head) in enumerate(heads):
            chosen = slice(at * spans, (at + 1) * spans)
            for place, (target, pair) in enumerate(
                ((out_ref, outputs[chosen]), (query_ref, query_grads[chosen]))
            ):
                first, second = pair
                target[0:CH, cols[inner]] = jnp.broadcast_to(first[CH - 1 :, :], (CH, HD)).astype(bf16)
                target[CH:, cols[inner]] = jnp.where(last, second[CH - 1 :, :], first).astype(bf16)
                back_ref[place * CH : (place + 1) * CH, cols[inner]] = second.astype(bf16)
            value = jnp.sum(terms[at * spans] + terms[at * spans + 1], axis=-1, keepdims=True)
            result = result + jnp.where(lane == head, value, 0.0)
        return result

    for at in range(0, HEADS_PER_STEP, SIDE_BY_SIDE):
        term_ref[...] += several(list(range(at, at + SIDE_BY_SIDE)))

    @pl.when(step == pl.num_programs(0) - 1)
    def _():
        for n in range(slots):
            row = row_sums(total_ref[n * NL : (n + 1) * NL, :])
            for device in range(project_ref.shape[0]):
                project_ref[device, n : n + 1, :] = row


def main_part(own_counts, head_gate, squares_all, gain, x, context, queries, out_grad, arrived, full_width):
    rows, width = x.shape
    heads = width // HD
    part = HEADS_PER_STEP * HD
    tokens = queries.shape[0]

    def tall(size, at=0):
        return pl.BlockSpec((size, part), lambda h: (at, h))

    smem = pl.BlockSpec(memory_space=pltpu.SMEM)
    whole = pl.BlockSpec(squares_all.shape, lambda h: (0, 0, 0))
    token_shape = jax.ShapeDtypeStruct((tokens, width), bf16)
    return pl.pallas_call(
        functools.partial(main_kernel, full_width),
        grid=(heads // HEADS_PER_STEP,),
        in_specs=[
            smem,
            smem,
            whole,
            pl.BlockSpec((1, part), lambda h: (0, h)),
            tall(rows),
            tall(tokens),
            tall(tokens),
            tall(tokens),
            tall(CH),
            tall(CH, 1),
        ],
        out_specs=[
            tall(rows),
            tall(tokens),
            tall(tokens),
            tall(tokens),
            tall(tokens),
            whole,
            pl.BlockSpec((1, HD), lambda h: (0, 0)),
        ],
        out_shape=[
            jax.ShapeDtypeStruct((rows, width), f32),
            token_shape,
            token_shape,
            token_shape,
            token_shape,
            jax.ShapeDtypeStruct(squares_all.shape, f32),
            jax.ShapeDtypeStruct((1, HD), f32),
        ],
        scratch_shapes=[pltpu.VMEM((rows, HD), f32), pltpu.VMEM((rows, HD), f32)],
        compiler_params=pltpu.CompilerParams(vmem_limit_bytes=VMEM_LIMIT),
        cost_estimate=cost(8 * 10**9, 10**7),
    )(own_counts, head_gate, squares_all, gain, x, context, queries, out_grad, arrived, arrived)


def final_kernel(
    full_width,
    square_ref,
    project_ref,
    x_ref,
    mid_ref,
    out_in_ref,
    query_in_ref,
    ret_out_ref,
    ret_query_ref,
    grad_ref,
    out_ref,
    query_ref,
    factor_ref,
):
    step = pl.program_id(0)
    slots = x_ref.shape[0] // NL

    @pl.when(step == 0)
    def _():
        inverse = inverse_rows(square_ref, full_width)
        project = (project_ref[0] + project_ref[1]) + (project_ref[2] + project_ref[3])
        factor = inverse * inverse * (project / full_width)
        for n in range(slots):
            factor_ref[n * NL : (n + 1) * NL, :] = columns(factor[n : n + 1, :])

    width = x_ref.shape[1]
    factor = factor_ref[...]
    for at in range(0, width, HD):
        cols = slice(at, at + HD)
        x = x_ref[:, cols].astype(f32)
        grad_ref[:, cols] = (mid_ref[:, cols] - x * factor).astype(bf16)
    last = lax.broadcasted_iota(jnp.int32, (CH, width), 0) == CH - 1
    for own, back, target in (
        (out_in_ref, ret_out_ref, out_ref),
        (query_in_ref, ret_query_ref, query_ref),
    ):
        own_rows = own[...].astype(f32)
        target[...] = jnp.where(last, own_rows, back[...].astype(f32)).astype(bf16)


def final(squares_all, projects_all, x, mid, out, query, returned, full_width):
    rows, width = x.shape
    tokens = out.shape[0]
    part = 2 * HD
    whole = pl.BlockSpec(squares_all.shape, lambda i: (0, 0, 0))
    tall = pl.BlockSpec((rows, part), lambda i: (0, i))
    half = pl.BlockSpec((CH, part), lambda i: (0, i))
    return pl.pallas_call(
        functools.partial(final_kernel, full_width),
        grid=(width // part,),
        in_specs=[
            whole,
            whole,
            tall,
            tall,
            half,
            half,
            half,
            pl.BlockSpec((CH, part), lambda i: (1, i)),
        ],
        out_specs=[tall, half, half],
        out_shape=[
            jax.ShapeDtypeStruct((rows, width), bf16),
            jax.ShapeDtypeStruct((tokens, width), bf16),
            jax.ShapeDtypeStruct((tokens, width), bf16),
        ],
        scratch_shapes=[pltpu.VMEM((rows, HD), f32)],
        input_output_aliases={4: 1, 5: 2},
        compiler_params=pltpu.CompilerParams(vmem_limit_bytes=VMEM_LIMIT),
        cost_estimate=cost(4 * rows * width, 8 * rows * width),
    )(squares_all, projects_all, x, mid, out, query, returned, returned)


def shards(queries, span_state, neigh_state, counts, norm_gain, head_gate, out_grad):
    head_count = head_gate.shape[0]
    width = queries.shape[1]
    row_count = queries.shape[0]
    span_count = row_count // CH
    ranks = lax.axis_size("tensor")
    full_width = float(ranks * width)
    lines = lax.axis_size("dp")

    local_squares, pack = squares(neigh_state, queries, out_grad, ranks)
    arrived = lax.ppermute(pack, "dp", [(i, i - 1) for i in range(1, lines)])
    squares_all = lax.all_to_all(local_squares, "tensor", 0, 0, tiled=True)
    gain = norm_gain[None, :]
    first_span = lax.axis_index("dp") * span_count
    own_counts = lax.dynamic_slice_in_dim(counts.reshape(-1), first_span, span_count)
    mid, out, query, back, context_grad, local_project, term = main_part(
        own_counts, head_gate, squares_all, gain, neigh_state, span_state, queries, out_grad,
        arrived, full_width,
    )
    everyone = lax.axis_size("group") * lines
    gathered = lax.all_to_all(
        jnp.broadcast_to(term, (everyone, HD)), ("group", "dp"), 0, 0, tiled=True
    )
    returned = lax.ppermute(back, "dp", [(i, i + 1) for i in range(lines - 1)])
    projects_all = lax.all_to_all(local_project, "tensor", 0, 0, tiled=True)
    summed = jnp.sum(gathered, axis=0)
    neighbour_grad, out, query = final(
        squares_all, projects_all, neigh_state, mid, out, query, returned, full_width
    )
    gate_tanh = jnp.tanh(head_gate)
    total_tokens = everyone * row_count
    gate_grad = (1.0 - gate_tanh * gate_tanh) * summed[:head_count] / math.sqrt(total_tokens)
    return out, query, context_grad, neighbour_grad, gate_grad


def solution(mesh):
    rows = P(("group", "dp"), "tensor")
    return jax.shard_map(
        shards,
        mesh=mesh,
        in_specs=(rows, rows, rows, P("group", None), P("tensor"), P("tensor"), rows),
        out_specs=(rows, rows, rows, rows, P("tensor")),
        check_vma=False,
    )
```

```python
import functools
import math

import jax
import jax.numpy as jnp
from jax import lax
from jax.experimental import pallas as pl
from jax.experimental.pallas import tpu as pltpu
from jax.sharding import PartitionSpec as P

CH = 64
NB = 2
NL = 128
HD = 128
KEYS = NL + CH
EPSILON = 1e-05
MASKED = -1e30
VMEM_LIMIT = 60 * 1024 * 1024
HEADS_PER_STEP = 4
SIDE_BY_SIDE = 4
SQUARE_BLOCKS = 2
FINAL_BLOCKS = 2

f32 = jnp.float32
bf16 = jnp.bfloat16


def dot(left, right, left_dim, right_dim):
    return lax.dot_general(
        left, right, (((left_dim,), (right_dim,)), ((), ())), preferred_element_type=f32
    )


def cost(flops, nbytes):
    return pl.CostEstimate(flops=flops, bytes_accessed=nbytes, transcendentals=0)


def columns(row):
    return jnp.transpose(jnp.broadcast_to(row, (NL, NL)))


def row_sums(block):
    return jnp.sum(jnp.transpose(block), axis=0, keepdims=True)


def inverse_rows(square_ref, full_width, at=slice(None)):
    return lax.rsqrt(square_ref[at, :] / full_width + EPSILON)


def squares_kernel(x_ref, q_ref, o_ref, sum_ref, pack_ref):
    step = pl.program_id(0)
    width = x_ref.shape[1]
    for n in range(SQUARE_BLOCKS):
        total = jnp.zeros((NL, HD), f32)
        for at in range(0, width, HD):
            part = x_ref[n * NL : (n + 1) * NL, at : at + HD].astype(f32)
            total = total + part * part
        sum_ref[pl.ds(step * SQUARE_BLOCKS + n, 1), :] = row_sums(total)

    @pl.when(step == 0)
    def _():
        pack_ref[:CH, :] = q_ref[...]
        pack_ref[CH:, :] = o_ref[...]


def squares(x, queries, out_grad):
    rows, width = x.shape
    count = rows // NL
    half = pl.BlockSpec((CH, width), lambda i: (0, 0))
    return pl.pallas_call(
        squares_kernel,
        grid=(count // SQUARE_BLOCKS,),
        in_specs=[pl.BlockSpec((SQUARE_BLOCKS * NL, width), lambda i: (i, 0)), half, half],
        out_specs=[
            pl.BlockSpec((count, NL), lambda i: (0, 0)),
            pl.BlockSpec((2 * CH, width), lambda i: (0, 0)),
        ],
        out_shape=[
            jax.ShapeDtypeStruct((count, NL), f32),
            jax.ShapeDtypeStruct((2 * CH, width), bf16),
        ],
        compiler_params=pltpu.CompilerParams(vmem_limit_bytes=VMEM_LIMIT),
        cost_estimate=cost(2 * rows * width, 2 * rows * width),
    )(x, queries, out_grad)


def cross(items):
    scale = 1.0 / math.sqrt(HD)
    lane = lax.broadcasted_iota(jnp.int32, (CH, NB * NL), 1)
    scores = [dot(block, keys, 1, 1) * scale for block, _, keys, _, _ in items]
    scores = [jnp.where(lane < it[3] * NL, sc, MASKED) for it, sc in zip(items, scores)]
    highest = [jnp.max(sc, axis=-1, keepdims=True) for sc in scores]
    powers = [jnp.exp(sc - hi) for sc, hi in zip(scores, highest)]
    sums = [jnp.sum(po, axis=-1, keepdims=True) for po in powers]
    weights = [po * (1.0 / su) for po, su in zip(powers, sums)]
    rounded = [we.astype(bf16) for we in weights]
    attended = [dot(ro, it[2], 1, 0) for it, ro in zip(items, rounded)]
    attended = [jnp.where(it[3] > 0, at, 0.0) for it, at in zip(items, attended)]
    att_grad = [jnp.where(it[3] > 0, it[4] * it[1], 0.0) for it in items]
    att_rounded = [ag.astype(bf16) for ag in att_grad]
    grad_weights = [dot(ar, it[2], 1, 1) for it, ar in zip(items, att_rounded)]
    offset = [jnp.sum(ag * at, axis=-1, keepdims=True) for ag, at in zip(att_grad, attended)]
    score_grad = [
        (we * (gw - of) * scale).astype(bf16) for we, gw, of in zip(weights, grad_weights, offset)
    ]
    query_grad = [dot(sg, it[2], 1, 0) for it, sg in zip(items, score_grad)]
    key_grad = [
        dot(
            jnp.concatenate([sg, ro], axis=0),
            jnp.concatenate([it[0], ar], axis=0),
            0,
            0,
        )
        for it, sg, ro, ar in zip(items, score_grad, rounded, att_rounded)
    ]
    outputs = [it[4] * at for it, at in zip(items, attended)]
    terms = [jnp.sum(it[1] * at, axis=0, keepdims=True) for it, at in zip(items, attended)]
    return outputs, query_grad, key_grad, terms


def main_kernel(
    full_width,
    counts_ref,
    gate_ref,
    square_ref,
    gain_ref,
    x_ref,
    context_ref,
    q_ref,
    o_ref,
    next_q_ref,
    next_o_ref,
    mid_ref,
    out_ref,
    query_ref,
    back_ref,
    context_grad_ref,
    project_ref,
    term_ref,
    inverse_ref,
    total_ref,
):
    step = pl.program_id(0)
    slots = x_ref.shape[0] // NL
    spans = slots // NB

    @pl.when(step == 0)
    def _():
        inverse = inverse_rows(square_ref, full_width)
        for n in range(slots):
            inverse_ref[n * NL : (n + 1) * NL, :] = columns(inverse[n : n + 1, :])
        total_ref[...] = jnp.zeros_like(total_ref)
        term_ref[...] = jnp.zeros_like(term_ref)

    last = lax.broadcasted_iota(jnp.int32, (CH, HD), 0) == CH - 1
    lane = lax.broadcasted_iota(jnp.int32, (1, HD), 1)
    first_span = lax.axis_index("dp") * spans

    def blocks(own_ref, next_ref, cols):
        own = own_ref[:, cols].astype(f32)
        following = next_ref[:, cols].astype(f32)
        first = jnp.where(last, own[CH - 1 : CH, :], own[CH:, :])
        second = jnp.where(last, own[2 * CH - 1 :, :], following)
        return first, second

    def several(inners):
        heads = [(inner, step * HEADS_PER_STEP + inner) for inner in inners]
        cols = {inner: slice(inner * HD, (inner + 1) * HD) for inner in inners}
        gains = {inner: gain_ref[:, cols[inner]] for inner in inners}
        gates = {inner: jnp.tanh(jnp.full((1, HD), gate_ref[head], f32)) for inner, head in heads}
        pairs = [(inner, n) for inner in inners for n in range(slots)]
        rows = [slice(n * NL, (n + 1) * NL) for n in range(slots)]
        xs = [x_ref[rows[n], cols[i]].astype(f32) for i, n in pairs]
        scaled = [x * inverse_ref[rows[n], :] for x, (i, n) in zip(xs, pairs)]
        normed = [(sc * gains[i]).astype(bf16) for sc, (i, n) in zip(scaled, pairs)]
        keys = [
            jnp.concatenate([no, context_ref[n // NB * CH : (n // NB + 1) * CH, cols[i]]], axis=0)
            for no, (i, n) in zip(normed, pairs)
        ]
        powers = [jnp.exp(dot(ke, no, 1, 1) * (1.0 / HD)) for ke, no in zip(keys, normed)]
        totals = [1.0 / jnp.sum(po, axis=0, keepdims=True) for po in powers]
        weights = [po * to for po, to in zip(powers, totals)]
        probs = [we.astype(bf16) for we in weights]
        encoded = [
            (x + dot(pr, ke, 0, 0)).astype(bf16) for x, pr, ke in zip(xs, probs, keys)
        ]
        items = []
        for inner in inners:
            q_blocks = blocks(q_ref, next_q_ref, cols[inner])
            o_blocks = blocks(o_ref, next_o_ref, cols[inner])
            for span in range(spans):
                first = inners.index(inner) * slots + span * NB
                items.append((
                    q_blocks[span].astype(bf16), o_blocks[span],
                    jnp.concatenate(encoded[first : first + NB], axis=0),
                    counts_ref[0, first_span + span], gates[inner],
                ))
        outputs, query_grads, span_grads, terms = cross(items)
        grads = [
            span_grads[k // NB][k % NB * NL : (k % NB + 1) * NL, :] for k in range(len(pairs))
        ]
        grad_rounded = [gr.astype(bf16) for gr in grads]
        grad_weights = [dot(ke, gr, 1, 1) for ke, gr in zip(keys, grad_rounded)]
        offsets = [jnp.sum(we * gw, axis=0, keepdims=True) for we, gw in zip(weights, grad_weights)]
        score_grads = [
            (we * (gw - of) * (1.0 / HD)).astype(bf16)
            for we, gw, of in zip(weights, grad_weights, offsets)
        ]
        key_grads = [
            dot(
                jnp.concatenate([sg, pr], axis=1),
                jnp.concatenate([no, gr], axis=0),
                1,
                0,
            )
            for sg, pr, no, gr in zip(score_grads, probs, normed, grad_rounded)
        ]
        gained = [
            (dot(sg, ke, 0, 0) + kg[:NL, :]) * gains[i]
            for sg, ke, kg, (i, n) in zip(score_grads, keys, key_grads, pairs)
        ]
        sums = [None] * slots
        for k, (i, n) in enumerate(pairs):
            product = gained[k] * scaled[k]
            sums[n] = product if sums[n] is None else sums[n] + product
            mid_ref[rows[n], cols[i]] = grads[k] + inverse_ref[rows[n], :] * gained[k]
            if n % NB == NB - 1:
                context_grad_ref[n // NB * CH : (n // NB + 1) * CH, cols[i]] = (
                    key_grads[k - 1][NL:, :] + key_grads[k][NL:, :]
                ).astype(bf16)
        for n in range(slots):
            total_ref[rows[n], :] += sums[n]
        result = jnp.zeros((1, HD), f32)
        for at, (inner, head) in enumerate(heads):
            chosen = slice(at * spans, (at + 1) * spans)
            for place, (target, pair) in enumerate(
                ((out_ref, outputs[chosen]), (query_ref, query_grads[chosen]))
            ):
                first, second = pair
                target[0:CH, cols[inner]] = jnp.broadcast_to(first[CH - 1 :, :], (CH, HD)).astype(bf16)
                target[CH:, cols[inner]] = jnp.where(last, second[CH - 1 :, :], first).astype(bf16)
                back_ref[place * CH : (place + 1) * CH, cols[inner]] = second.astype(bf16)
            value = jnp.sum(terms[at * spans] + terms[at * spans + 1], axis=-1, keepdims=True)
            result = result + jnp.where(lane == head, value, 0.0)
        return result

    for at in range(0, HEADS_PER_STEP, SIDE_BY_SIDE):
        term_ref[...] += several(list(range(at, at + SIDE_BY_SIDE)))

    @pl.when(step == pl.num_programs(0) - 1)
    def _():
        for n in range(slots):
            row = row_sums(total_ref[n * NL : (n + 1) * NL, :])
            for peer in range(project_ref.shape[0]):
                project_ref[peer, n : n + 1, :] = row


def main_part(counts, head_gate, squares_all, gain, x, context, queries, out_grad, arrived, full_width, ranks):
    rows, width = x.shape
    heads = width // HD
    part = HEADS_PER_STEP * HD
    tokens = queries.shape[0]

    def tall(size, at=0):
        return pl.BlockSpec((size, part), lambda h: (at, h))

    smem = pl.BlockSpec(memory_space=pltpu.SMEM)
    whole = pl.BlockSpec(squares_all.shape, lambda h: (0, 0))
    token_shape = jax.ShapeDtypeStruct((tokens, width), bf16)
    return pl.pallas_call(
        functools.partial(main_kernel, full_width),
        grid=(heads // HEADS_PER_STEP,),
        in_specs=[
            smem,
            smem,
            whole,
            pl.BlockSpec((1, part), lambda h: (0, h)),
            tall(rows),
            tall(tokens),
            tall(tokens),
            tall(tokens),
            tall(CH),
            tall(CH, 1),
        ],
        out_specs=[
            tall(rows),
            tall(tokens),
            tall(tokens),
            tall(tokens),
            tall(tokens),
            pl.BlockSpec((ranks,) + squares_all.shape, lambda h: (0, 0, 0)),
            pl.BlockSpec((1, HD), lambda h: (0, 0)),
        ],
        out_shape=[
            jax.ShapeDtypeStruct((rows, width), f32),
            token_shape,
            token_shape,
            token_shape,
            token_shape,
            jax.ShapeDtypeStruct((ranks,) + squares_all.shape, f32),
            jax.ShapeDtypeStruct((1, HD), f32),
        ],
        scratch_shapes=[pltpu.VMEM((rows, HD), f32), pltpu.VMEM((rows, HD), f32)],
        compiler_params=pltpu.CompilerParams(vmem_limit_bytes=VMEM_LIMIT),
        cost_estimate=cost(8 * 10**9, 10**7),
    )(counts, head_gate, squares_all, gain, x, context, queries, out_grad, arrived, arrived)


def final_kernel(
    full_width,
    square_ref,
    project_ref,
    x_ref,
    mid_ref,
    out_in_ref,
    query_in_ref,
    ret_out_ref,
    ret_query_ref,
    gate_ref,
    grad_ref,
    out_ref,
    query_ref,
    slope_ref,
    *,
    slope_scale,
):
    step = pl.program_id(0)
    gate_tanh = jnp.tanh(gate_ref[...])
    slope_ref[...] = (1.0 - gate_tanh * gate_tanh) * slope_scale
    width = x_ref.shape[1]
    for n in range(FINAL_BLOCKS):
        row = pl.ds(step * FINAL_BLOCKS + n, 1)
        inverse = inverse_rows(square_ref, full_width, row)
        one, two, three, four = (project_ref[at, row, :] for at in range(4))
        project = (one + two) + (three + four)
        factor = columns(inverse * inverse * (project / full_width))
        rows = slice(n * NL, (n + 1) * NL)
        for at in range(0, width, HD):
            cols = slice(at, at + HD)
            x = x_ref[rows, cols].astype(f32)
            grad_ref[rows, cols] = (mid_ref[rows, cols] - x * factor).astype(bf16)
    last = lax.broadcasted_iota(jnp.int32, (CH, out_ref.shape[1]), 0) == CH - 1
    for own, back, target in (
        (out_in_ref, ret_out_ref, out_ref),
        (query_in_ref, ret_query_ref, query_ref),
    ):
        own_rows = own[...].astype(f32)
        target[...] = jnp.where(last, own_rows, back[...].astype(f32)).astype(bf16)


def final(
    squares_all, projects_all, x, mid, out, query, returned, head_gate, full_width, scale
):
    rows, width = x.shape
    tokens = out.shape[0]
    count = rows // NL // FINAL_BLOCKS
    part = width // count
    gate = pl.BlockSpec(head_gate.shape, lambda i: (0, 0))
    whole = pl.BlockSpec(squares_all.shape, lambda i: (0, 0))
    rowwise = pl.BlockSpec((FINAL_BLOCKS * NL, width), lambda i: (i, 0))
    half = pl.BlockSpec((CH, part), lambda i: (0, i))
    return pl.pallas_call(
        functools.partial(final_kernel, full_width, slope_scale=scale),
        grid=(count,),
        in_specs=[
            whole,
            pl.BlockSpec(projects_all.shape, lambda i: (0, 0, 0)),
            rowwise,
            rowwise,
            half,
            half,
            half,
            pl.BlockSpec((CH, part), lambda i: (1, i)),
            gate,
        ],
        out_specs=[rowwise, half, half, gate],
        out_shape=[
            jax.ShapeDtypeStruct((rows, width), bf16),
            jax.ShapeDtypeStruct((tokens, width), bf16),
            jax.ShapeDtypeStruct((tokens, width), bf16),
            jax.ShapeDtypeStruct(head_gate.shape, f32),
        ],
        input_output_aliases={4: 1, 5: 2},
        compiler_params=pltpu.CompilerParams(vmem_limit_bytes=VMEM_LIMIT),
        cost_estimate=cost(4 * rows * width, 8 * rows * width),
    )(squares_all, projects_all, x, mid, out, query, returned, returned, head_gate)


def gate_kernel(slope_ref, terms_ref, grad_ref):
    heads = grad_ref.shape[1]
    total = jnp.sum(terms_ref[...], axis=0)
    grad_ref[...] = slope_ref[...] * total[:, :heads]


def gate_part(slope, terms):
    return pl.pallas_call(
        gate_kernel,
        out_shape=jax.ShapeDtypeStruct(slope.shape, f32),
        compiler_params=pltpu.CompilerParams(vmem_limit_bytes=16 * 1024 * 1024),
        cost_estimate=cost(1000, 1000),
    )(slope, terms)


def shards(queries, span_state, neigh_state, counts, norm_gain, head_gate, out_grad):
    head_count = head_gate.shape[0]
    width = queries.shape[1]
    row_count = queries.shape[0]
    full_width = float(lax.axis_size("tensor") * width)
    lines = lax.axis_size("dp")

    local_squares, pack = squares(neigh_state, queries, out_grad)
    squares_all = lax.psum(local_squares, "tensor")
    arrived = lax.ppermute(pack, "dp", [(i, i - 1) for i in range(1, lines)])
    mid, out, query, back, context_grad, project, term = main_part(
        counts, head_gate, squares_all, norm_gain[None, :], neigh_state, span_state, queries,
        out_grad, arrived, full_width, lax.axis_size("tensor"),
    )
    projects_all = lax.all_to_all(project, "tensor", 0, 0, tiled=True)
    returned = lax.ppermute(back, "dp", [(i, i + 1) for i in range(lines - 1)])
    line_terms = jnp.broadcast_to(lax.psum(term, "group"), (lines, 1, HD))
    terms = lax.all_to_all(line_terms, "dp", 0, 0, tiled=True)
    neighbour_grad, out, query, slope = final(
        squares_all, projects_all, neigh_state, mid, out, query, returned, head_gate[None, :],
        full_width, 1.0 / math.sqrt(lax.axis_size("group") * lines * row_count),
    )
    gate_grad = gate_part(slope, terms)[0]
    return out, query, context_grad, neighbour_grad, gate_grad


def solution(mesh):
    rows = P(("group", "dp"), "tensor")
    return jax.shard_map(
        shards,
        mesh=mesh,
        in_specs=(rows, rows, rows, P("group", None), P("tensor"), P("tensor"), rows),
        out_specs=(rows, rows, rows, rows, P("tensor")),
        check_vma=False,
    )
```

```python
import functools
import math

import jax
import jax.numpy as jnp
from jax import lax
from jax.experimental import pallas as pl
from jax.experimental.pallas import tpu as pltpu
from jax.sharding import PartitionSpec as P

CH = 64
NB = 2
NL = 128
HD = 128
KEYS = NL + CH
EPSILON = 1e-05
MASKED = -1e30
VMEM_LIMIT = 60 * 1024 * 1024
MAIN_LIMIT = 61440 * 1024
FINAL_LIMIT = 54528 * 1024
HEADS_PER_STEP = 4
SIDE_BY_SIDE = 4
SQUARE_BLOCKS = 2
FINAL_BLOCKS = 2

f32 = jnp.float32
bf16 = jnp.bfloat16


def dot(left, right, left_dim, right_dim):
    return lax.dot_general(
        left, right, (((left_dim,), (right_dim,)), ((), ())), preferred_element_type=f32
    )


def cost(flops, nbytes):
    return pl.CostEstimate(flops=flops, bytes_accessed=nbytes, transcendentals=0)


def columns(row):
    return jnp.transpose(jnp.broadcast_to(row, (NL, NL)))


def row_sums(block):
    return jnp.sum(jnp.transpose(block), axis=0, keepdims=True)


def inverse_rows(square_ref, full_width, at=slice(None)):
    return lax.rsqrt(square_ref[at, :] / full_width + EPSILON)


def squares_kernel(x_ref, q_ref, o_ref, sum_ref, pack_ref):
    step = pl.program_id(0)
    width = x_ref.shape[1]
    for n in range(SQUARE_BLOCKS):
        total = jnp.zeros((NL, HD), f32)
        for at in range(0, width, HD):
            part = x_ref[n * NL : (n + 1) * NL, at : at + HD].astype(f32)
            total = total + part * part
        sum_ref[pl.ds(step * SQUARE_BLOCKS + n, 1), :] = row_sums(total)

    @pl.when(step == 0)
    def _():
        pack_ref[:CH, :] = q_ref[...]
        pack_ref[CH:, :] = o_ref[...]


def squares(x, queries, out_grad):
    rows, width = x.shape
    count = rows // NL
    half = pl.BlockSpec((CH, width), lambda i: (0, 0))
    return pl.pallas_call(
        squares_kernel,
        grid=(count // SQUARE_BLOCKS,),
        in_specs=[pl.BlockSpec((SQUARE_BLOCKS * NL, width), lambda i: (i, 0)), half, half],
        out_specs=[
            pl.BlockSpec((count, NL), lambda i: (0, 0)),
            pl.BlockSpec((2 * CH, width), lambda i: (0, 0)),
        ],
        out_shape=[
            jax.ShapeDtypeStruct((count, NL), f32),
            jax.ShapeDtypeStruct((2 * CH, width), bf16),
        ],
        compiler_params=pltpu.CompilerParams(vmem_limit_bytes=VMEM_LIMIT),
        cost_estimate=cost(2 * rows * width, 2 * rows * width),
    )(x, queries, out_grad)


def cross(items):
    scale = 1.0 / math.sqrt(HD)
    lane = lax.broadcasted_iota(jnp.int32, (CH, NB * NL), 1)
    scores = [dot(block, keys, 1, 1) * scale for block, _, keys, _, _ in items]
    weights, rounded = [], []
    for it, score in zip(items, scores):
        score = jnp.where(lane < it[3] * NL, score, MASKED)
        powers = jnp.exp(score - jnp.max(score, axis=-1, keepdims=True))
        weights.append(powers * (1.0 / jnp.sum(powers, axis=-1, keepdims=True)))
        rounded.append(weights[-1].astype(bf16))
    attended = [dot(ro, it[2], 1, 0) for it, ro in zip(items, rounded)]
    attended = [jnp.where(it[3] > 0, at, 0.0) for it, at in zip(items, attended)]
    att_grad = [jnp.where(it[3] > 0, it[4] * it[1], 0.0) for it in items]
    att_rounded = [ag.astype(bf16) for ag in att_grad]
    grad_weights = [dot(ar, it[2], 1, 1) for it, ar in zip(items, att_rounded)]
    offset = [jnp.sum(ag * at, axis=-1, keepdims=True) for ag, at in zip(att_grad, attended)]
    score_grad = [
        (we * (gw - of) * scale).astype(bf16) for we, gw, of in zip(weights, grad_weights, offset)
    ]
    query_grad = [dot(sg, it[2], 1, 0) for it, sg in zip(items, score_grad)]
    key_grad = [
        dot(
            jnp.concatenate([sg, ro], axis=0),
            jnp.concatenate([it[0], ar], axis=0),
            0,
            0,
        )
        for it, sg, ro, ar in zip(items, score_grad, rounded, att_rounded)
    ]
    outputs = [it[4] * at for it, at in zip(items, attended)]
    terms = [jnp.sum(it[1] * at, axis=0, keepdims=True) for it, at in zip(items, attended)]
    return outputs, query_grad, key_grad, terms


def main_kernel(
    full_width,
    counts_ref,
    gate_ref,
    square_ref,
    gain_ref,
    x_ref,
    context_ref,
    q_ref,
    o_ref,
    next_q_ref,
    next_o_ref,
    mid_ref,
    out_ref,
    query_ref,
    back_ref,
    context_grad_ref,
    project_ref,
    term_ref,
    inverse_ref,
    total_ref,
):
    step = pl.program_id(0)
    slots = x_ref.shape[0] // NL
    spans = slots // NB

    @pl.when(step == 0)
    def _():
        inverse = inverse_rows(square_ref, full_width)
        for n in range(slots):
            inverse_ref[n * NL : (n + 1) * NL, :] = columns(inverse[n : n + 1, :])
        total_ref[...] = jnp.zeros_like(total_ref)
        term_ref[...] = jnp.zeros_like(term_ref)

    last = lax.broadcasted_iota(jnp.int32, (CH, HD), 0) == CH - 1
    lane = lax.broadcasted_iota(jnp.int32, (1, HD), 1)
    first_span = lax.axis_index("dp") * spans

    def blocks(own_ref, next_ref, cols):
        own = own_ref[:, cols].astype(f32)
        following = next_ref[:, cols].astype(f32)
        first = jnp.where(last, own[CH - 1 : CH, :], own[CH:, :])
        second = jnp.where(last, own[2 * CH - 1 :, :], following)
        return first, second

    def several(inners):
        heads = [(inner, step * HEADS_PER_STEP + inner) for inner in inners]
        cols = {inner: slice(inner * HD, (inner + 1) * HD) for inner in inners}
        gains = {inner: gain_ref[:, cols[inner]] for inner in inners}
        gates = {inner: jnp.tanh(jnp.full((1, HD), gate_ref[head], f32)) for inner, head in heads}
        pairs = [(inner, n) for inner in inners for n in range(slots)]
        rows = [slice(n * NL, (n + 1) * NL) for n in range(slots)]
        xs = [x_ref[rows[n], cols[i]].astype(f32) for i, n in pairs]
        scaled = [x * inverse_ref[rows[n], :] for x, (i, n) in zip(xs, pairs)]
        normed = [(sc * gains[i]).astype(bf16) for sc, (i, n) in zip(scaled, pairs)]
        keys = [
            jnp.concatenate([no, context_ref[n // NB * CH : (n // NB + 1) * CH, cols[i]]], axis=0)
            for no, (i, n) in zip(normed, pairs)
        ]
        scores = [dot(ke, no, 1, 1) for ke, no in zip(keys, normed)]
        weights, probs = [], []
        for score in scores:
            powers = jnp.exp(score * (1.0 / HD))
            weights.append(powers * (1.0 / jnp.sum(powers, axis=0, keepdims=True)))
            probs.append(weights[-1].astype(bf16))
        encoded = [
            (x + dot(pr, ke, 0, 0)).astype(bf16) for x, pr, ke in zip(xs, probs, keys)
        ]
        items = []
        for inner in inners:
            q_blocks = blocks(q_ref, next_q_ref, cols[inner])
            o_blocks = blocks(o_ref, next_o_ref, cols[inner])
            for span in range(spans):
                first = inners.index(inner) * slots + span * NB
                items.append((
                    q_blocks[span].astype(bf16), o_blocks[span],
                    jnp.concatenate(encoded[first : first + NB], axis=0),
                    counts_ref[0, first_span + span], gates[inner],
                ))
        outputs, query_grads, span_grads, terms = cross(items)
        grads = [
            span_grads[k // NB][k % NB * NL : (k % NB + 1) * NL, :] for k in range(len(pairs))
        ]
        grad_rounded = [gr.astype(bf16) for gr in grads]
        grad_weights = [dot(ke, gr, 1, 1) for ke, gr in zip(keys, grad_rounded)]
        score_grads = []
        for we, gw in zip(weights, grad_weights):
            offset = jnp.sum(we * gw, axis=0, keepdims=True)
            score_grads.append((we * (gw - offset) * (1.0 / HD)).astype(bf16))
        key_grads = [
            dot(
                jnp.concatenate([sg, pr], axis=1),
                jnp.concatenate([no, gr], axis=0),
                1,
                0,
            )
            for sg, pr, no, gr in zip(score_grads, probs, normed, grad_rounded)
        ]
        gained = [
            (dot(sg, ke, 0, 0) + kg[:NL, :]) * gains[i]
            for sg, ke, kg, (i, n) in zip(score_grads, keys, key_grads, pairs)
        ]
        sums = [None] * slots
        for k, (i, n) in enumerate(pairs):
            product = gained[k] * scaled[k]
            sums[n] = product if sums[n] is None else sums[n] + product
            mid_ref[rows[n], cols[i]] = grads[k] + inverse_ref[rows[n], :] * gained[k]
            if n % NB == NB - 1:
                context_grad_ref[n // NB * CH : (n // NB + 1) * CH, cols[i]] = (
                    key_grads[k - 1][NL:, :] + key_grads[k][NL:, :]
                ).astype(bf16)
        for n in range(slots):
            total_ref[rows[n], :] += sums[n]
        result = jnp.zeros((1, HD), f32)
        for at, (inner, head) in enumerate(heads):
            chosen = slice(at * spans, (at + 1) * spans)
            for place, (target, pair) in enumerate(
                ((out_ref, outputs[chosen]), (query_ref, query_grads[chosen]))
            ):
                first, second = pair
                target[0:CH, cols[inner]] = jnp.broadcast_to(first[CH - 1 :, :], (CH, HD)).astype(bf16)
                target[CH:, cols[inner]] = jnp.where(last, second[CH - 1 :, :], first).astype(bf16)
                back_ref[place * CH : (place + 1) * CH, cols[inner]] = second.astype(bf16)
            value = jnp.sum(terms[at * spans] + terms[at * spans + 1], axis=-1, keepdims=True)
            result = result + jnp.where(lane == head, value, 0.0)
        return result

    for at in range(0, HEADS_PER_STEP, SIDE_BY_SIDE):
        term_ref[...] += several(list(range(at, at + SIDE_BY_SIDE)))

    @pl.when(step == pl.num_programs(0) - 1)
    def _():
        for n in range(slots):
            row = row_sums(total_ref[n * NL : (n + 1) * NL, :])
            project_ref[n : n + 1, :] = row


def main_part(counts, head_gate, squares_all, gain, x, context, queries, out_grad, arrived, full_width):
    rows, width = x.shape
    heads = width // HD
    part = HEADS_PER_STEP * HD
    tokens = queries.shape[0]

    def tall(size, at=0):
        return pl.BlockSpec((size, part), lambda h: (at, h))

    smem = pl.BlockSpec(memory_space=pltpu.SMEM)
    whole = pl.BlockSpec(squares_all.shape, lambda h: (0, 0))
    token_shape = jax.ShapeDtypeStruct((tokens, width), bf16)
    return pl.pallas_call(
        functools.partial(main_kernel, full_width),
        grid=(heads // HEADS_PER_STEP,),
        in_specs=[
            smem,
            smem,
            whole,
            pl.BlockSpec((1, part), lambda h: (0, h)),
            tall(rows),
            tall(tokens),
            tall(tokens),
            tall(tokens),
            tall(CH),
            tall(CH, 1),
        ],
        out_specs=[
            tall(rows),
            tall(tokens),
            tall(tokens),
            tall(tokens),
            tall(tokens),
            whole,
            pl.BlockSpec((1, HD), lambda h: (0, 0)),
        ],
        out_shape=[
            jax.ShapeDtypeStruct((rows, width), f32),
            token_shape,
            token_shape,
            token_shape,
            token_shape,
            jax.ShapeDtypeStruct(squares_all.shape, f32),
            jax.ShapeDtypeStruct((1, HD), f32),
        ],
        scratch_shapes=[pltpu.VMEM((rows, HD), f32), pltpu.VMEM((rows, HD), f32)],
        compiler_params=pltpu.CompilerParams(vmem_limit_bytes=MAIN_LIMIT),
        cost_estimate=cost(8 * 10**9, 10**7),
    )(counts, head_gate, squares_all, gain, x, context, queries, out_grad, arrived, arrived)


def final_kernel(
    full_width,
    square_ref,
    project_ref,
    x_ref,
    mid_ref,
    out_in_ref,
    query_in_ref,
    ret_out_ref,
    ret_query_ref,
    gate_ref,
    terms_ref,
    grad_ref,
    out_ref,
    query_ref,
    gate_grad_ref,
    *,
    scale,
):
    step = pl.program_id(0)
    gate_tanh = jnp.tanh(gate_ref[...])
    summed = jnp.sum(terms_ref[...], axis=0)[:, : gate_tanh.shape[1]]
    gate_grad_ref[...] = (1.0 - gate_tanh * gate_tanh) * summed * scale
    width = x_ref.shape[1]
    for n in range(FINAL_BLOCKS):
        row = pl.ds(step * FINAL_BLOCKS + n, 1)
        inverse = inverse_rows(square_ref, full_width, row)
        project = project_ref[row, :]
        factor = columns(inverse * inverse * (project / full_width))
        rows = slice(n * NL, (n + 1) * NL)
        for at in range(0, width, HD):
            cols = slice(at, at + HD)
            x = x_ref[rows, cols].astype(f32)
            grad_ref[rows, cols] = (mid_ref[rows, cols] - x * factor).astype(bf16)
    last = lax.broadcasted_iota(jnp.int32, (CH, out_ref.shape[1]), 0) == CH - 1
    for own, back, target in (
        (out_in_ref, ret_out_ref, out_ref),
        (query_in_ref, ret_query_ref, query_ref),
    ):
        own_rows = own[...].astype(f32)
        target[...] = jnp.where(last, own_rows, back[...].astype(f32)).astype(bf16)


def final(
    squares_all, projects_all, x, mid, out, query, returned, head_gate, terms, full_width, scale
):
    rows, width = x.shape
    tokens = out.shape[0]
    count = rows // NL // FINAL_BLOCKS
    part = width // count
    gate = pl.BlockSpec(head_gate.shape, lambda i: (0, 0))
    whole = pl.BlockSpec(squares_all.shape, lambda i: (0, 0))
    rowwise = pl.BlockSpec((FINAL_BLOCKS * NL, width), lambda i: (i, 0))
    half = pl.BlockSpec((CH, part), lambda i: (0, i))
    return pl.pallas_call(
        functools.partial(final_kernel, full_width, scale=scale),
        grid=(count,),
        in_specs=[
            whole,
            pl.BlockSpec(projects_all.shape, lambda i: (0, 0)),
            rowwise,
            rowwise,
            half,
            half,
            half,
            pl.BlockSpec((CH, part), lambda i: (1, i)),
            gate,
            pl.BlockSpec(terms.shape, lambda i: (0, 0, 0)),
        ],
        out_specs=[rowwise, half, half, gate],
        out_shape=[
            jax.ShapeDtypeStruct((rows, width), bf16),
            jax.ShapeDtypeStruct((tokens, width), bf16),
            jax.ShapeDtypeStruct((tokens, width), bf16),
            jax.ShapeDtypeStruct(head_gate.shape, f32),
        ],
        input_output_aliases={4: 1, 5: 2},
        compiler_params=pltpu.CompilerParams(vmem_limit_bytes=FINAL_LIMIT),
        cost_estimate=cost(4 * rows * width, 8 * rows * width),
    )(squares_all, projects_all, x, mid, out, query, returned, returned, head_gate, terms)


def shards(queries, span_state, neigh_state, counts, norm_gain, head_gate, out_grad):
    width = queries.shape[1]
    row_count = queries.shape[0]
    full_width = float(lax.axis_size("tensor") * width)
    lines = lax.axis_size("dp")

    local_squares, pack = squares(neigh_state, queries, out_grad)
    squares_all = lax.psum(local_squares, "tensor")
    arrived = lax.ppermute(pack, "dp", [(i, i - 1) for i in range(1, lines)])
    mid, out, query, back, context_grad, project, term = main_part(
        counts, head_gate, squares_all, norm_gain[None, :], neigh_state, span_state, queries,
        out_grad, arrived, full_width,
    )
    returned = lax.ppermute(back, "dp", [(i, i + 1) for i in range(lines - 1)])
    line_terms = jnp.broadcast_to(lax.psum(term, "group"), (lines, 1, HD))
    line_terms, project = lax.optimization_barrier((line_terms, project))
    terms = lax.all_to_all(line_terms, "dp", 0, 0, tiled=True)
    projects_all = lax.psum(project, "tensor")
    neighbour_grad, out, query, gate_grad = final(
        squares_all, projects_all, neigh_state, mid, out, query, returned, head_gate[None, :],
        terms,
        full_width, 1.0 / math.sqrt(lax.axis_size("group") * lines * row_count),
    )
    return out, query, context_grad, neighbour_grad, gate_grad[0]


def solution(mesh):
    rows = P(("group", "dp"), "tensor")
    return jax.shard_map(
        shards,
        mesh=mesh,
        in_specs=(rows, rows, rows, P("group", None), P("tensor"), P("tensor"), rows),
        out_specs=(rows, rows, rows, rows, P("tensor")),
        check_vma=False,
    )
```

```python
import functools
import math

import jax
import jax.numpy as jnp
from jax import lax
from jax.experimental import pallas as pl
from jax.experimental.pallas import tpu as pltpu
from jax.sharding import PartitionSpec as P

CH = 64
NB = 2
NL = 128
HD = 128
KEYS = NL + CH
EPSILON = 1e-05
MASKED = -1e30
VMEM_LIMIT = 60 * 1024 * 1024
MAIN_LIMIT = 62144 * 1024
FINAL_LIMIT = 54528 * 1024
HEADS_PER_STEP = 4
SIDE_BY_SIDE = 4
SQUARE_BLOCKS = 2
FINAL_BLOCKS = 2

f32 = jnp.float32
bf16 = jnp.bfloat16


def dot(left, right, left_dim, right_dim):
    return lax.dot_general(
        left, right, (((left_dim,), (right_dim,)), ((), ())), preferred_element_type=f32
    )


def cost(flops, nbytes):
    return pl.CostEstimate(flops=flops, bytes_accessed=nbytes, transcendentals=0)


def columns(row):
    return jnp.transpose(jnp.broadcast_to(row, (NL, NL)))


def row_sums(block):
    return jnp.sum(jnp.transpose(block), axis=0, keepdims=True)


def inverse_rows(square_ref, full_width, at=slice(None)):
    return lax.rsqrt(square_ref[at, :] / full_width + EPSILON)


def squares_kernel(x_ref, q_ref, o_ref, sum_ref, pack_ref):
    step = pl.program_id(0)
    width = x_ref.shape[1]
    for n in range(SQUARE_BLOCKS):
        total = jnp.zeros((NL, HD), f32)
        for at in range(0, width, HD):
            part = x_ref[n * NL : (n + 1) * NL, at : at + HD].astype(f32)
            total = total + part * part
        sum_ref[pl.ds(step * SQUARE_BLOCKS + n, 1), :] = row_sums(total)

    @pl.when(step == 0)
    def _():
        pack_ref[:CH, :] = q_ref[...]
        pack_ref[CH:, :] = o_ref[...]


def squares(x, queries, out_grad):
    rows, width = x.shape
    count = rows // NL
    half = pl.BlockSpec((CH, width), lambda i: (0, 0))
    return pl.pallas_call(
        squares_kernel,
        grid=(count // SQUARE_BLOCKS,),
        in_specs=[pl.BlockSpec((SQUARE_BLOCKS * NL, width), lambda i: (i, 0)), half, half],
        out_specs=[
            pl.BlockSpec((count, NL), lambda i: (0, 0)),
            pl.BlockSpec((2 * CH, width), lambda i: (0, 0)),
        ],
        out_shape=[
            jax.ShapeDtypeStruct((count, NL), f32),
            jax.ShapeDtypeStruct((2 * CH, width), bf16),
        ],
        compiler_params=pltpu.CompilerParams(vmem_limit_bytes=VMEM_LIMIT),
        cost_estimate=cost(2 * rows * width, 2 * rows * width),
    )(x, queries, out_grad)


def cross(items):
    scale = 1.0 / math.sqrt(HD)
    lane = lax.broadcasted_iota(jnp.int32, (CH, NB * NL), 1)
    scores = [dot(block, keys, 1, 1) * scale for block, _, keys, _, _ in items]
    weights, rounded = [], []
    for it, score in zip(items, scores):
        score = jnp.where(lane < it[3] * NL, score, MASKED)
        powers = jnp.exp(score - jnp.max(score, axis=-1, keepdims=True))
        weights.append(powers * (1.0 / jnp.sum(powers, axis=-1, keepdims=True)))
        rounded.append(weights[-1].astype(bf16))
    attended = [dot(ro, it[2], 1, 0) for it, ro in zip(items, rounded)]
    attended = [jnp.where(it[3] > 0, at, 0.0) for it, at in zip(items, attended)]
    att_grad = [jnp.where(it[3] > 0, it[4] * it[1], 0.0) for it in items]
    att_rounded = [ag.astype(bf16) for ag in att_grad]
    grad_weights = [dot(ar, it[2], 1, 1) for it, ar in zip(items, att_rounded)]
    offset = [jnp.sum(ag * at, axis=-1, keepdims=True) for ag, at in zip(att_grad, attended)]
    score_grad = [
        (we * (gw - of) * scale).astype(bf16) for we, gw, of in zip(weights, grad_weights, offset)
    ]
    query_grad = [dot(sg, it[2], 1, 0) for it, sg in zip(items, score_grad)]
    key_grad = [
        dot(
            jnp.concatenate([sg, ro], axis=0),
            jnp.concatenate([it[0], ar], axis=0),
            0,
            0,
        )
        for it, sg, ro, ar in zip(items, score_grad, rounded, att_rounded)
    ]
    outputs = [it[4] * at for it, at in zip(items, attended)]
    terms = [jnp.sum(it[1] * at, axis=0, keepdims=True) for it, at in zip(items, attended)]
    return outputs, query_grad, key_grad, terms


def main_kernel(
    full_width,
    counts_ref,
    gate_ref,
    square_ref,
    gain_ref,
    x_ref,
    context_ref,
    q_ref,
    o_ref,
    next_q_ref,
    next_o_ref,
    mid_ref,
    out_ref,
    query_ref,
    back_ref,
    context_grad_ref,
    project_ref,
    term_ref,
    inverse_ref,
    total_ref,
):
    step = pl.program_id(0)
    slots = x_ref.shape[0] // NL
    spans = slots // NB

    @pl.when(step == 0)
    def _():
        inverse = inverse_rows(square_ref, full_width)
        for n in range(slots):
            inverse_ref[n * NL : (n + 1) * NL, :] = columns(inverse[n : n + 1, :])
        total_ref[...] = jnp.zeros_like(total_ref)
        term_ref[...] = jnp.zeros_like(term_ref)

    last = lax.broadcasted_iota(jnp.int32, (CH, HD), 0) == CH - 1
    lane = lax.broadcasted_iota(jnp.int32, (1, HD), 1)
    first_span = lax.axis_index("dp") * spans

    def blocks(own_ref, next_ref, cols):
        own = own_ref[:, cols].astype(f32)
        following = next_ref[:, cols].astype(f32)
        first = jnp.where(last, own[CH - 1 : CH, :], own[CH:, :])
        second = jnp.where(last, own[2 * CH - 1 :, :], following)
        return first, second

    def several(inners):
        heads = [(inner, step * HEADS_PER_STEP + inner) for inner in inners]
        cols = {inner: slice(inner * HD, (inner + 1) * HD) for inner in inners}
        gains = {inner: gain_ref[:, cols[inner]] for inner in inners}
        gates = {inner: jnp.tanh(jnp.full((1, HD), gate_ref[head], f32)) for inner, head in heads}
        pairs = [(inner, n) for inner in inners for n in range(slots)]
        rows = [slice(n * NL, (n + 1) * NL) for n in range(slots)]
        xs = [x_ref[rows[n], cols[i]].astype(f32) for i, n in pairs]
        scaled = [x * inverse_ref[rows[n], :] for x, (i, n) in zip(xs, pairs)]
        normed = [(sc * gains[i]).astype(bf16) for sc, (i, n) in zip(scaled, pairs)]
        keys = [
            jnp.concatenate([no, context_ref[n // NB * CH : (n // NB + 1) * CH, cols[i]]], axis=0)
            for no, (i, n) in zip(normed, pairs)
        ]
        scores = [dot(ke, no, 1, 1) for ke, no in zip(keys, normed)]
        weights, probs = [], []
        for score in scores:
            powers = jnp.exp(score * (1.0 / HD))
            weights.append(powers * (1.0 / jnp.sum(powers, axis=0, keepdims=True)))
            probs.append(weights[-1].astype(bf16))
        encoded = [
            (x + dot(pr, ke, 0, 0)).astype(bf16) for x, pr, ke in zip(xs, probs, keys)
        ]
        items = []
        for inner in inners:
            q_blocks = blocks(q_ref, next_q_ref, cols[inner])
            o_blocks = blocks(o_ref, next_o_ref, cols[inner])
            for span in range(spans):
                first = inners.index(inner) * slots + span * NB
                items.append((
                    q_blocks[span].astype(bf16), o_blocks[span],
                    jnp.concatenate(encoded[first : first + NB], axis=0),
                    counts_ref[0, first_span + span], gates[inner],
                ))
        outputs, query_grads, span_grads, terms = cross(items)
        grads = [
            span_grads[k // NB][k % NB * NL : (k % NB + 1) * NL, :] for k in range(len(pairs))
        ]
        grad_rounded = [gr.astype(bf16) for gr in grads]
        grad_weights = [dot(ke, gr, 1, 1) for ke, gr in zip(keys, grad_rounded)]
        score_grads = []
        for we, gw in zip(weights, grad_weights):
            offset = jnp.sum(we * gw, axis=0, keepdims=True)
            score_grads.append((we * (gw - offset) * (1.0 / HD)).astype(bf16))
        key_grads = [
            dot(
                jnp.concatenate([sg, pr], axis=1),
                jnp.concatenate([no, gr], axis=0),
                1,
                0,
            )
            for sg, pr, no, gr in zip(score_grads, probs, normed, grad_rounded)
        ]
        gained = [
            (dot(sg, ke, 0, 0) + kg[:NL, :]) * gains[i]
            for sg, ke, kg, (i, n) in zip(score_grads, keys, key_grads, pairs)
        ]
        sums = [None] * slots
        for k, (i, n) in enumerate(pairs):
            product = gained[k] * scaled[k]
            sums[n] = product if sums[n] is None else sums[n] + product
            mid_ref[rows[n], cols[i]] = (grads[k] + inverse_ref[rows[n], :] * gained[k]).astype(bf16)
            if n % NB == NB - 1:
                context_grad_ref[n // NB * CH : (n // NB + 1) * CH, cols[i]] = (
                    key_grads[k - 1][NL:, :] + key_grads[k][NL:, :]
                ).astype(bf16)
        for n in range(slots):
            total_ref[rows[n], :] += sums[n]
        result = jnp.zeros((1, HD), f32)
        for at, (inner, head) in enumerate(heads):
            chosen = slice(at * spans, (at + 1) * spans)
            for place, (target, pair) in enumerate(
                ((out_ref, outputs[chosen]), (query_ref, query_grads[chosen]))
            ):
                first, second = pair
                target[0:CH, cols[inner]] = jnp.broadcast_to(first[CH - 1 :, :], (CH, HD)).astype(bf16)
                target[CH:, cols[inner]] = jnp.where(last, second[CH - 1 :, :], first).astype(bf16)
                back_ref[place * CH : (place + 1) * CH, cols[inner]] = second.astype(bf16)
            value = jnp.sum(terms[at * spans] + terms[at * spans + 1], axis=-1, keepdims=True)
            result = result + jnp.where(lane == head, value, 0.0)
        return result

    for at in range(0, HEADS_PER_STEP, SIDE_BY_SIDE):
        term_ref[...] += several(list(range(at, at + SIDE_BY_SIDE)))

    @pl.when(step == pl.num_programs(0) - 1)
    def _():
        for n in range(slots):
            row = row_sums(total_ref[n * NL : (n + 1) * NL, :])
            project_ref[n : n + 1, :] = row


def main_part(counts, head_gate, squares_all, gain, x, context, queries, out_grad, arrived, full_width):
    rows, width = x.shape
    heads = width // HD
    part = HEADS_PER_STEP * HD
    tokens = queries.shape[0]

    def tall(size, at=0):
        return pl.BlockSpec((size, part), lambda h: (at, h))

    smem = pl.BlockSpec(memory_space=pltpu.SMEM)
    whole = pl.BlockSpec(squares_all.shape, lambda h: (0, 0))
    token_shape = jax.ShapeDtypeStruct((tokens, width), bf16)
    return pl.pallas_call(
        functools.partial(main_kernel, full_width),
        grid=(heads // HEADS_PER_STEP,),
        in_specs=[
            smem,
            smem,
            whole,
            pl.BlockSpec((1, part), lambda h: (0, h)),
            tall(rows),
            tall(tokens),
            tall(tokens),
            tall(tokens),
            tall(CH),
            tall(CH, 1),
        ],
        out_specs=[
            tall(rows),
            tall(tokens),
            tall(tokens),
            tall(tokens),
            tall(tokens),
            whole,
            pl.BlockSpec((1, HD), lambda h: (0, 0)),
        ],
        out_shape=[
            jax.ShapeDtypeStruct((rows, width), bf16),
            token_shape,
            token_shape,
            token_shape,
            token_shape,
            jax.ShapeDtypeStruct(squares_all.shape, f32),
            jax.ShapeDtypeStruct((1, HD), f32),
        ],
        scratch_shapes=[pltpu.VMEM((rows, HD), f32), pltpu.VMEM((rows, HD), f32)],
        compiler_params=pltpu.CompilerParams(vmem_limit_bytes=MAIN_LIMIT),
        cost_estimate=cost(8 * 10**9, 10**7),
    )(counts, head_gate, squares_all, gain, x, context, queries, out_grad, arrived, arrived)


def final_kernel(
    full_width,
    square_ref,
    project_ref,
    x_ref,
    mid_ref,
    out_in_ref,
    query_in_ref,
    ret_out_ref,
    ret_query_ref,
    gate_ref,
    terms_ref,
    grad_ref,
    out_ref,
    query_ref,
    gate_grad_ref,
    *,
    scale,
):
    step = pl.program_id(0)
    gate_tanh = jnp.tanh(gate_ref[...])
    summed = jnp.sum(terms_ref[...], axis=0)[:, : gate_tanh.shape[1]]
    gate_grad_ref[...] = (1.0 - gate_tanh * gate_tanh) * summed * scale
    width = x_ref.shape[1]
    for n in range(FINAL_BLOCKS):
        row = pl.ds(step * FINAL_BLOCKS + n, 1)
        inverse = inverse_rows(square_ref, full_width, row)
        project = project_ref[row, :]
        factor = columns(inverse * inverse * (project / full_width))
        rows = slice(n * NL, (n + 1) * NL)
        for at in range(0, width, HD):
            cols = slice(at, at + HD)
            x = x_ref[rows, cols].astype(f32)
            grad_ref[rows, cols] = (mid_ref[rows, cols].astype(f32) - x * factor).astype(bf16)
    last = lax.broadcasted_iota(jnp.int32, (CH, out_ref.shape[1]), 0) == CH - 1
    for own, back, target in (
        (out_in_ref, ret_out_ref, out_ref),
        (query_in_ref, ret_query_ref, query_ref),
    ):
        own_rows = own[...].astype(f32)
        target[...] = jnp.where(last, own_rows, back[...].astype(f32)).astype(bf16)


def final(
    squares_all, projects_all, x, mid, out, query, returned, head_gate, terms, full_width, scale
):
    rows, width = x.shape
    tokens = out.shape[0]
    count = rows // NL // FINAL_BLOCKS
    part = width // count
    gate = pl.BlockSpec(head_gate.shape, lambda i: (0, 0))
    whole = pl.BlockSpec(squares_all.shape, lambda i: (0, 0))
    rowwise = pl.BlockSpec((FINAL_BLOCKS * NL, width), lambda i: (i, 0))
    half = pl.BlockSpec((CH, part), lambda i: (0, i))
    return pl.pallas_call(
        functools.partial(final_kernel, full_width, scale=scale),
        grid=(count,),
        in_specs=[
            whole,
            pl.BlockSpec(projects_all.shape, lambda i: (0, 0)),
            rowwise,
            rowwise,
            half,
            half,
            half,
            pl.BlockSpec((CH, part), lambda i: (1, i)),
            gate,
            pl.BlockSpec(terms.shape, lambda i: (0, 0, 0)),
        ],
        out_specs=[rowwise, half, half, gate],
        out_shape=[
            jax.ShapeDtypeStruct((rows, width), bf16),
            jax.ShapeDtypeStruct((tokens, width), bf16),
            jax.ShapeDtypeStruct((tokens, width), bf16),
            jax.ShapeDtypeStruct(head_gate.shape, f32),
        ],
        input_output_aliases={4: 1, 5: 2},
        compiler_params=pltpu.CompilerParams(vmem_limit_bytes=FINAL_LIMIT),
        cost_estimate=cost(4 * rows * width, 8 * rows * width),
    )(squares_all, projects_all, x, mid, out, query, returned, returned, head_gate, terms)


def shards(queries, span_state, neigh_state, counts, norm_gain, head_gate, out_grad):
    width = queries.shape[1]
    row_count = queries.shape[0]
    full_width = float(lax.axis_size("tensor") * width)
    lines = lax.axis_size("dp")

    local_squares, pack = squares(neigh_state, queries, out_grad)
    squares_all = lax.psum(local_squares, "tensor")
    arrived = lax.ppermute(pack, "dp", [(i, i - 1) for i in range(1, lines)])
    mid, out, query, back, context_grad, project, term = main_part(
        counts, head_gate, squares_all, norm_gain[None, :], neigh_state, span_state, queries,
        out_grad, arrived, full_width,
    )
    returned = lax.ppermute(back, "dp", [(i, i + 1) for i in range(lines - 1)])
    line_terms = jnp.broadcast_to(lax.psum(term, "group"), (lines, 1, HD))
    line_terms, project = lax.optimization_barrier((line_terms, project))
    terms = lax.all_to_all(line_terms, "dp", 0, 0, tiled=True)
    projects_all = lax.psum(project, "tensor")
    neighbour_grad, out, query, gate_grad = final(
        squares_all, projects_all, neigh_state, mid, out, query, returned, head_gate[None, :],
        terms,
        full_width, 1.0 / math.sqrt(lax.axis_size("group") * lines * row_count),
    )
    return out, query, context_grad, neighbour_grad, gate_grad[0]


def solution(mesh):
    rows = P(("group", "dp"), "tensor")
    return jax.shard_map(
        shards,
        mesh=mesh,
        in_specs=(rows, rows, rows, P("group", None), P("tensor"), P("tensor"), rows),
        out_specs=(rows, rows, rows, rows, P("tensor")),
        check_vma=False,
    )
```
